32 devices in a mesh: seq: 8 (over y, x, core), mp: 4 (over z).
Axes of the slice: x: 2, y: 2, z: 4, core: 2. Of those that a mesh axis runs over, the one named last changes fastest.
Arguments:
- byte_values: int32 [8192], P('seq'), may hold values from 0 to 255
- hash_owner: int32 [8192, 1], P('seq'), may hold values from 0 to 7; in each aligned block of 1024 rows (0 to 1023, 1024 to 2047, ...) at most 256 rows name the same one
- hash_slot: int32 [8192], P('seq'), may hold values from 0 to 4095
- patch_start: int32 [256], P('seq'), may hold values from 0 to 8191, as said below
- byte_table: bfloat16 [256, 1280], P(None, 'mp'), may hold values from -6 to 6
- hash_table: bfloat16 [32768, 1280], P('seq', 'mp'), may hold values from -6 to 6
- norm_gains: float32 [3, 1280], replicated, may hold values from 0.5 to 1.5
- w_query: bfloat16 [1280, 1280], P(None, 'mp'), may hold values from -8 to 8
- w_key: bfloat16 [1280, 1280], P(None, 'mp'), may hold values from -8 to 8
- w_value: bfloat16 [1280, 1280], P(None, 'mp'), may hold values from -0.15625 to 0.15625
- w_attn_out: bfloat16 [1280, 1280], P('mp'), may hold values from -0.15625 to 0.15625
- w_gate: bfloat16 [1280, 3584], P('seq', 'mp'), may hold values from -0.15625 to 0.15625
- w_up: bfloat16 [1280, 3584], P('seq', 'mp'), may hold values from -0.15625 to 0.15625
- w_down: bfloat16 [3584, 1280], P('mp', 'seq'), may hold values from -0.09375 to 0.09375
- w_cross_query: bfloat16 [1280, 1280], P(None, 'mp'), may hold values from -8 to 8
- w_cross_key: bfloat16 [1280, 1280], P(None, 'mp'), may hold values from -8 to 8
- w_cross_value: bfloat16 [1280, 1280], P(None, 'mp'), may hold values from -0.15625 to 0.15625
- w_cross_out: bfloat16 [1280, 1280], P('mp'), may hold values from -0.15625 to 0.15625
- w_global: bfloat16 [1280, 4096], P(None, 'mp'), may hold values from -0.15625 to 0.15625
Outputs:
- patches: bfloat16 [256, 4096], P('seq', 'mp')
The draws below stay inside these ranges and needn't reach their ends.
Inputs may be any that keep to these rules, and one draw needn't show every extreme that they name: `hash_owner`: in each aligned block of 1024 rows (the bytes of one range) every value is named by at most 256 bytes; in some blocks one value is named by exactly 256 bytes. patch_start rises strictly and begins with 0. The patches p with p // 32 = s start at or after s * 1024 - 512 and end at or before (s + 1) * 1024 + 512; in every draw some group starts exactly 512 bytes before its range and some group ends exactly 512 bytes after its range.
All inputs are finite; a program needn't handle non-finite values.
Results may differ from the reference program's by a relative error of at most 0.025.
Values may be sent and summed in bfloat16 or wider, within the bound.
A program may use at most 128 MiB of HBM per device.

```python
import math
import jax
import jax.numpy as jnp
import numpy as np
from jax import lax

D = 1280
HEADS = 20
HD = 64
FF = 3584
GD = 4096
WINDOW = 512
HROW_DEV = 4096
BYTES_DEV = 1024
PATCH_DEV = 32
REACH = 512
BYTES = 8192
NPATCH = 256
HASH_ROWS = 32768
CAP = 256
N_SEQ = 8
N_MP = 4


def query_key_pair(key, salt):
    base = jax.random.fold_in(key, salt)
    first_key, second_key = jax.random.split(base, 2)
    key_weight = jax.random.normal(first_key, (D, D), jnp.float32) * D ** (-0.5)
    noise = jax.random.normal(second_key, (D, D), jnp.float32) * D ** (-0.5)
    query_weight = noise
    return (query_weight, key_weight)


def draw_w_query(key, part):
    return query_key_pair(key, 11)[0].astype(jnp.bfloat16)


def draw_w_key(key, part):
    return query_key_pair(key, 11)[1].astype(jnp.bfloat16)


def draw_w_cross_query(key, part):
    return query_key_pair(key, 23)[0].astype(jnp.bfloat16)


def draw_w_cross_key(key, part):
    return query_key_pair(key, 23)[1].astype(jnp.bfloat16)


def draw_patch_start(key, part):
    owners = BYTES // BYTES_DEV
    base = jax.random.fold_in(key, 29)
    first_key, second_key, third_key, fourth_key = jax.random.split(base, 4)
    raw = jax.random.randint(first_key, (owners,), -(REACH - PATCH_DEV), REACH - PATCH_DEV + 1)
    low_at = jax.random.randint(second_key, (), 0, owners - 1)
    offset = jax.random.randint(third_key, (), 0, owners - 3)
    high_at = (low_at + 1 + offset) % (owners - 1)
    index = jnp.arange(owners, dtype=jnp.int32)
    drift = jnp.where(index == low_at, -REACH, raw)
    drift = jnp.where(index == high_at, REACH, drift)
    drift = jnp.where(index == owners - 1, 0, drift)
    previous = jnp.concatenate([jnp.zeros((1,), jnp.int32), drift[:-1]])
    totals = BYTES_DEV + drift - previous
    weights = jax.random.randint(fourth_key, (owners, PATCH_DEV), 1, 17)
    running = jnp.cumsum(weights, axis=1)
    whole = running[:, -1:]
    spare = (totals - PATCH_DEV)[:, None]
    cuts = spare * running // whole
    earlier_cuts = jnp.concatenate([jnp.zeros((owners, 1), jnp.int32), cuts[:, :-1]], axis=1)
    lengths = 1 + cuts - earlier_cuts
    inner = jnp.cumsum(lengths, axis=1) - lengths
    owner_start = index * BYTES_DEV + previous
    return (owner_start[:, None] + inner).reshape(-1).astype(jnp.int32)


def plant(entries, stream_key, low, high):
    longest = entries.shape.index(max(entries.shape))
    spots = []
    for shift in (0, 1):
        where = [jax.random.randint(jax.random.fold_in(stream_key, axis), (), 0, length) for axis, length in enumerate(entries.shape)]
        where[longest] = (where[longest] + shift) % entries.shape[longest]
        spots.append(tuple(where))
    return entries.at[spots[0]].set(low).at[spots[1]].set(high)


def level_of(key, extent, pieces, least, top_value):
    factor_of, own = 1.0, jax.random.fold_in(key, 6)
    for position, blocks in pieces:
        steps = jnp.exp(jax.random.uniform(jax.random.fold_in(own, position), (blocks,), jnp.float32, least / len(pieces), top_value / len(pieces)))
        factor_of = factor_of * jnp.repeat(steps, extent[position] // blocks).reshape([-1 if axis == position else 1 for axis in range(len(extent))])
    return factor_of


def rank_table(number_of, skew):
    loads = [(1 << 20) // math.isqrt(rank ** skew) + 1 for rank in range(1, number_of + 1)]
    scale = 1 + sum(loads) // (1 << 30)
    return np.cumsum(np.array([max(1, weight // scale) for weight in loads]))


def ranked(stream_key, dims, number_of, slope):
    table = rank_table(number_of, slope)
    ticket = jax.random.randint(jax.random.fold_in(stream_key, 1), dims, 0, int(table[number_of - 1]))
    grade = jnp.searchsorted(jnp.asarray(table, jnp.int32), ticket, side="right")
    return jax.random.permutation(jax.random.fold_in(stream_key, 2), number_of)[grade].astype(jnp.int32)


def routed_block(stream_key, own, number, rows, count, top, most, slope):
    order = jax.random.permutation(stream_key, count)
    crowded, usual = portions_of(count, rows * top, most, slope, True), portions_of(count, rows * top, most, slope, False)
    places = jnp.arange(count)

    def named(sizes, turn):
        used = int((sizes > 0).sum())
        fixed = max(1, used // 4)
        moved = fixed + (places - fixed + turn * (used - fixed)) % max(1, count - fixed)
        return jnp.zeros((count,), jnp.int32).at[order[jnp.where(places < fixed, places, moved)]].set(jnp.asarray(sizes, jnp.int32))

    sizes = jnp.where(number % 4 == 0, named(crowded, number // 4), named(usual, number - number // 4 - 1))
    mixed = jax.random.permutation(jax.random.fold_in(own, 3), count)
    donor, sink = mixed[0:count // 2 * 2:2], mixed[1:count // 2 * 2:2]
    margin = jnp.minimum(sizes[donor] - 1, most - sizes[sink]) // 2
    margin = jnp.where((donor == order[0]) | (sink == order[0]) | (sizes[sink] == 0), 0, jnp.maximum(margin, 0))
    moved = jax.random.randint(jax.random.fold_in(own, 4), (count // 2,), 0, 1 << 20) % (margin + 1)
    sizes = sizes.at[donor].add(-moved).at[sink].add(moved)
    items = jnp.searchsorted(jnp.cumsum(sizes), jnp.arange(rows * top), side="right").astype(jnp.int32)
    listing = items.reshape(top, rows).T
    listing = listing[jax.random.permutation(jax.random.fold_in(own, 1), rows)]
    turn = jax.random.randint(jax.random.fold_in(own, 2), (rows, 1), 0, top)
    return jnp.take_along_axis(listing, (jnp.arange(top)[None, :] + turn) % top, axis=1)


def portions_of(number_of, total, limit, skew, full):
    weights = [(1 << 20) // math.isqrt(rank ** skew) + 1 for rank in range(1, number_of + 1)]
    largest = limit if full else min(limit, max(-(-total // number_of), total * weights[0] // sum(weights)))
    least = 1 if total - largest >= number_of - 1 else 0
    given, rest = [largest] + [least] * (number_of - 1), total - largest - least * (number_of - 1)
    while rest > 0:
        free = [i for i in range(1, number_of) if given[i] < largest] or [i for i in range(1, number_of) if given[i] < limit]
        whole, left = sum([weights[i] for i in free]), rest
        for i in free:
            extra = min(limit - given[i], max(1, left * weights[i] // whole), rest)
            given[i] = given[i] + extra
            rest = rest - extra
    return np.array(given)


def normal_values(key, shape, spread, limit, pieces=(), held_as=jnp.bfloat16):
    result = jax.random.normal(key, shape, jnp.float32) * spread
    if len(pieces) > 0:
        result = level_of(key, shape, pieces, -0.22, 0.18) * result
    return jnp.clip(result, min=-limit, max=limit).astype(held_as)


def setup_inputs(seed: int = 0) -> dict:
    streams_of = jax.random.split(jax.random.key(seed), 20)
    byte_values = plant(ranked(streams_of[0], (BYTES,), 256, 2), jax.random.fold_in(streams_of[0], 3), 0, 255).astype(jnp.int32)
    hash_owner_keys = jax.random.split(jax.random.fold_in(streams_of[1], 1), BYTES // BYTES_DEV)
    hash_owner_turns = jax.random.permutation(jax.random.fold_in(streams_of[1], 3), BYTES // BYTES_DEV)
    hash_owner = jax.vmap(lambda own, number: routed_block(jax.random.fold_in(streams_of[1], 2), own, number, BYTES_DEV, BYTES // BYTES_DEV, 1, CAP, 2))(hash_owner_keys, hash_owner_turns).reshape((BYTES, 1))
    hash_slot = plant(jax.random.randint(streams_of[2], (BYTES,), 0, HROW_DEV), jax.random.fold_in(streams_of[2], 1), 0, HROW_DEV - 1).astype(jnp.int32)
    patch_start = draw_patch_start(jax.random.fold_in(streams_of[19], 71), 0)
    byte_table = normal_values(streams_of[4], (256, D), 1.0, 6.0, ((1, 4),))
    hash_table = normal_values(streams_of[5], (HASH_ROWS, D), 1.0, 6.0, ((0, 8), (1, 4)))
    norm_gains = jnp.clip(1.0 + 0.1 * jax.random.normal(streams_of[6], (3, D), jnp.float32), 0.5, 1.5)
    w_query = draw_w_query(jax.random.fold_in(streams_of[19], 71), 0)
    w_key = draw_w_key(jax.random.fold_in(streams_of[19], 71), 0)
    w_value = normal_values(streams_of[9], (D, D), D ** -0.5, 0.15625, ((1, 4),))
    w_attn_out = normal_values(streams_of[10], (D, D), D ** -0.5, 0.15625, ((0, 4),))
    w_gate = normal_values(streams_of[11], (D, FF), D ** -0.5, 0.15625, ((0, 8), (1, 4)))
    w_up = normal_values(streams_of[12], (D, FF), D ** -0.5, 0.15625, ((0, 8), (1, 4)))
    w_down = normal_values(streams_of[13], (FF, D), FF ** -0.5, 0.09375, ((0, 4), (1, 8)))
    w_cross_query = draw_w_cross_query(jax.random.fold_in(streams_of[19], 71), 0)
    w_cross_key = draw_w_cross_key(jax.random.fold_in(streams_of[19], 71), 0)
    w_cross_value = normal_values(streams_of[16], (D, D), D ** -0.5, 0.15625, ((1, 4),))
    w_cross_out = normal_values(streams_of[17], (D, D), D ** -0.5, 0.15625, ((0, 4),))
    w_global = normal_values(streams_of[18], (D, GD), D ** -0.5, 0.15625, ((1, 4),))
    return dict(byte_values=byte_values, hash_owner=hash_owner, hash_slot=hash_slot, patch_start=patch_start, byte_table=byte_table, hash_table=hash_table, norm_gains=norm_gains, w_query=w_query, w_key=w_key, w_value=w_value, w_attn_out=w_attn_out, w_gate=w_gate, w_up=w_up, w_down=w_down, w_cross_query=w_cross_query, w_cross_key=w_cross_key, w_cross_value=w_cross_value, w_cross_out=w_cross_out, w_global=w_global)


def rms_scale(values, gain):
    return values * lax.rsqrt(lax.optimization_barrier(jnp.mean(values * values, axis=-1, keepdims=True)) + 1e-05) * gain

def rounded(values):
    return lax.optimization_barrier(values.astype(jnp.bfloat16)).astype(jnp.float32)

def masked_softmax(scores, valid):
    scores = jnp.where(valid, scores, -1e+30)
    highest = lax.optimization_barrier(jnp.max(scores, axis=-1, keepdims=True))
    raised = jnp.exp(scores - highest)
    return raised / lax.optimization_barrier(jnp.sum(raised, axis=-1, keepdims=True))

def grouped_sum(left, right, groups):
    width = left.shape[1] // groups
    total = jnp.zeros((left.shape[0], right.shape[1]), jnp.float32)
    for group in range(groups):
        term = jnp.dot(left[:, group * width:(group + 1) * width], right[group * width:(group + 1) * width], preferred_element_type=jnp.float32)
        total = total + rounded(term)
    return total

def reference(byte_values, hash_owner, hash_slot, patch_start, byte_table, hash_table, norm_gains, w_query, w_key, w_value, w_attn_out, w_gate, w_up, w_down, w_cross_query, w_cross_key, w_cross_value, w_cross_out, w_global):
    row_ids = (hash_owner[:, 0] * HROW_DEV + hash_slot).astype(jnp.int32)
    hash_rows = jnp.take(hash_table, row_ids, axis=0).astype(jnp.float32)
    byte_rows = jnp.take(byte_table, byte_values, axis=0).astype(jnp.float32)
    embed = (byte_rows + hash_rows).astype(jnp.bfloat16)
    residual = embed.astype(jnp.float32)
    normed = rms_scale(residual, norm_gains[0]).astype(jnp.bfloat16)
    queries = jnp.dot(normed, w_query, preferred_element_type=jnp.float32).astype(jnp.bfloat16)
    keys = jnp.dot(normed, w_key, preferred_element_type=jnp.float32).astype(jnp.bfloat16)
    values = jnp.dot(normed, w_value, preferred_element_type=jnp.float32).astype(jnp.bfloat16)
    padding = jnp.zeros((WINDOW, D), jnp.bfloat16)
    key_span = jnp.concatenate([padding, keys], axis=0)
    value_span = jnp.concatenate([padding, values], axis=0)

    def attend(block):
        start = block * WINDOW
        query_block = lax.dynamic_slice_in_dim(queries, start, WINDOW, 0).astype(jnp.float32).reshape(WINDOW, HEADS, HD)
        key_block = lax.dynamic_slice_in_dim(key_span, start, 2 * WINDOW, 0).astype(jnp.float32).reshape(2 * WINDOW, HEADS, HD)
        value_block = lax.dynamic_slice_in_dim(value_span, start, 2 * WINDOW, 0).astype(jnp.float32).reshape(2 * WINDOW, HEADS, HD)
        query_pos = start + jnp.arange(WINDOW, dtype=jnp.int32)
        key_pos = start - WINDOW + jnp.arange(2 * WINDOW, dtype=jnp.int32)
        valid = (key_pos[None, :] <= query_pos[:, None]) & (key_pos[None, :] > query_pos[:, None] - WINDOW) & (key_pos[None, :] >= 0)
        scores = jnp.einsum('qhd,khd->hqk', query_block, key_block) * HD ** (-0.5)
        weights = rounded(masked_softmax(scores, valid[None]))
        mixed = jnp.einsum('hqk,khd->qhd', weights, value_block)
        return mixed.astype(jnp.bfloat16).reshape(WINDOW, D)
    heads_out = lax.map(attend, jnp.arange(BYTES // WINDOW, dtype=jnp.int32)).reshape(BYTES, D)
    residual = residual + grouped_sum(heads_out, w_attn_out, N_MP)
    normed = rms_scale(residual, norm_gains[1]).astype(jnp.bfloat16)

    def feed_forward(block_rows):
        gate = jnp.dot(block_rows, w_gate, preferred_element_type=jnp.float32)
        lifted = jnp.dot(block_rows, w_up, preferred_element_type=jnp.float32)
        hidden = (jax.nn.silu(gate) * lifted).astype(jnp.bfloat16)
        return grouped_sum(hidden, w_down, N_MP)
    residual = residual + lax.map(feed_forward, normed.reshape(N_SEQ, BYTES_DEV, D)).reshape(BYTES, D)
    encoded = rms_scale(residual, norm_gains[2]).astype(jnp.bfloat16)
    cross_keys = jnp.dot(encoded, w_cross_key, preferred_element_type=jnp.float32).astype(jnp.bfloat16)
    cross_values = jnp.dot(encoded, w_cross_value, preferred_element_type=jnp.float32).astype(jnp.bfloat16)
    framed_states = jnp.pad(encoded, ((REACH, REACH), (0, 0)))
    framed_keys = jnp.pad(cross_keys, ((REACH, REACH), (0, 0)))
    framed_values = jnp.pad(cross_values, ((REACH, REACH), (0, 0)))
    patch_end = jnp.concatenate([patch_start[1:], jnp.full((1,), BYTES, dtype=jnp.int32)])
    frame_len = BYTES_DEV + 2 * REACH

    def pool(owner):
        first = owner * BYTES_DEV
        states = lax.dynamic_slice_in_dim(framed_states, first, frame_len, 0)
        frame_keys = lax.dynamic_slice_in_dim(framed_keys, first, frame_len, 0).astype(jnp.float32).reshape(frame_len, HEADS, HD)
        frame_values = lax.dynamic_slice_in_dim(framed_values, first, frame_len, 0).astype(jnp.float32).reshape(frame_len, HEADS, HD)
        starts = lax.dynamic_slice_in_dim(patch_start, owner * PATCH_DEV, PATCH_DEV, 0)
        stops = lax.dynamic_slice_in_dim(patch_end, owner * PATCH_DEV, PATCH_DEV, 0)
        frame_pos = first - REACH + jnp.arange(frame_len, dtype=jnp.int32)
        member = (frame_pos[None, :] >= starts[:, None]) & (frame_pos[None, :] < stops[:, None])
        counts = lax.optimization_barrier(jnp.sum(member.astype(jnp.float32), axis=1))
        pooled = jnp.dot(member.astype(jnp.bfloat16), states, preferred_element_type=jnp.float32) / counts[:, None]
        pooled_rows = pooled.astype(jnp.bfloat16)
        cross_queries = rounded(jnp.dot(pooled_rows, w_cross_query, preferred_element_type=jnp.float32)).reshape(PATCH_DEV, HEADS, HD)
        scores = jnp.einsum('phd,khd->hpk', cross_queries, frame_keys) * HD ** (-0.5)
        weights = rounded(masked_softmax(scores, member[None]))
        cross_heads = jnp.einsum('hpk,khd->phd', weights, frame_values).astype(jnp.bfloat16).reshape(PATCH_DEV, D)
        mixed = jnp.dot(cross_heads, w_cross_out, preferred_element_type=jnp.float32)
        patch_hidden = (pooled + mixed).astype(jnp.bfloat16)
        return jnp.dot(patch_hidden, w_global, preferred_element_type=jnp.float32).astype(jnp.bfloat16)
    return lax.map(pool, jnp.arange(N_SEQ, dtype=jnp.int32)).reshape(NPATCH, GD)
```

```python
import jax
import jax.numpy as jnp
from jax import lax
from jax.sharding import PartitionSpec as P

HD = 64
WINDOW = 512
REACH = 512


def passed_along(value, axis, steps):
    count = lax.axis_size(axis)
    first, last = (max(0, -steps), min(count, count - steps))
    return lax.ppermute(value, axis, [(source, source + steps) for source in range(first, last)])


def padded(cells, sides, width):
    for axis, dim in sides:
        count = lax.axis_size(axis)
        ends = count - 1
        head = lax.slice_in_dim(cells, 0, width, axis=dim)
        tail = lax.slice_in_dim(cells, cells.shape[dim] - width, cells.shape[dim], axis=dim)
        cells = jnp.concatenate(
            [
                lax.ppermute(tail, axis, [(i, (i + 1) % count) for i in range(ends)]),
                cells,
                lax.ppermute(head, axis, [((i + 1) % count, i) for i in range(ends)]),
            ],
            axis=dim,
        )
    return cells


def rms_scale(values, gain):
    return values * lax.rsqrt(jnp.mean(values * values, axis=-1, keepdims=True) + 1e-05) * gain


def masked_softmax(scores, valid):
    scores = jnp.where(valid, scores, -1e30)
    highest = jnp.max(scores, axis=-1, keepdims=True)
    raised = jnp.exp(scores - highest)
    return raised / jnp.sum(raised, axis=-1, keepdims=True)


def per_device(
    byte_values,
    hash_owner,
    hash_slot,
    patch_start,
    byte_table,
    hash_table,
    norm_gains,
    w_query,
    w_key,
    w_value,
    w_attn_out,
    w_gate,
    w_up,
    w_down,
    w_cross_query,
    w_cross_key,
    w_cross_value,
    w_cross_out,
    w_global,
):
    seq_count = lax.axis_size("seq")
    position = lax.axis_index("seq")
    length = byte_values.shape[0]
    local_width = w_query.shape[1]
    local_heads = local_width // HD
    capacity = 2 * length // seq_count
    owner = hash_owner[:, 0]
    owner_hot = (owner[:, None] == jnp.arange(seq_count, dtype=jnp.int32)[None, :]).astype(
        jnp.bfloat16
    )
    line = jnp.arange(length, dtype=jnp.int32)
    earlier = (line[:, None] > line[None, :]).astype(jnp.bfloat16)
    before = jnp.dot(earlier, owner_hot, preferred_element_type=jnp.float32)
    order = jnp.sum(before * owner_hot.astype(jnp.float32), axis=1).astype(jnp.int32)
    target = owner * capacity + order
    chosen = (target[:, None] == jnp.arange(seq_count * capacity, dtype=jnp.int32)[None, :]).astype(
        jnp.bfloat16
    )
    digits = jnp.stack([hash_slot // 64, hash_slot % 64], axis=0).astype(jnp.bfloat16)
    asked = jnp.dot(digits, chosen, preferred_element_type=jnp.float32).astype(jnp.int32)
    requests = (asked[0] * 64 + asked[1]).reshape(seq_count, capacity)
    wanted = lax.all_to_all(requests, "seq", split_axis=0, concat_axis=0, tiled=True).reshape(-1)
    picked = (
        wanted[:, None] == jnp.arange(hash_table.shape[0], dtype=jnp.int32)[None, :]
    ).astype(jnp.bfloat16)
    found = jnp.dot(picked, hash_table, preferred_element_type=jnp.float32).astype(jnp.bfloat16)
    fetched = lax.all_to_all(
        found.reshape(seq_count, capacity, -1), "seq", split_axis=0, concat_axis=0, tiled=True
    ).reshape(seq_count * capacity, -1)
    hash_rows = jnp.dot(chosen, fetched, preferred_element_type=jnp.float32)
    byte_hot = (byte_values[:, None] == jnp.arange(256, dtype=jnp.int32)[None, :]).astype(
        jnp.bfloat16
    )
    byte_rows = jnp.dot(byte_hot, byte_table, preferred_element_type=jnp.float32)
    embed = (byte_rows + hash_rows).astype(jnp.bfloat16)
    full_gate = lax.all_gather(w_gate, "seq", axis=0, tiled=True)
    full_up = lax.all_gather(w_up, "seq", axis=0, tiled=True)
    full_down = lax.all_gather(w_down, "seq", axis=1, tiled=True)
    embed, full_gate, full_up, full_down = lax.optimization_barrier(
        (embed, full_gate, full_up, full_down)
    )
    embed_parts = lax.all_gather(embed, "mp", axis=0, tiled=False)
    embed_full = jnp.concatenate(
        [embed_parts[i] for i in range(embed_parts.shape[0])], axis=1
    )
    share = length // lax.axis_size("mp")
    residual = lax.dynamic_slice_in_dim(
        embed_full, lax.axis_index("mp") * share, share, axis=0
    ).astype(jnp.float32)
    layer_in = rms_scale(embed_full.astype(jnp.float32), norm_gains[0]).astype(jnp.bfloat16)
    queries = jnp.dot(layer_in, w_query, preferred_element_type=jnp.float32).astype(jnp.bfloat16)
    keys = jnp.dot(layer_in, w_key, preferred_element_type=jnp.float32).astype(jnp.bfloat16)
    values = jnp.dot(layer_in, w_value, preferred_element_type=jnp.float32).astype(jnp.bfloat16)
    paired = jnp.stack([keys, values])
    earlier_pair = passed_along(paired[:, length - WINDOW :], "seq", 1)
    key_span = jnp.concatenate([earlier_pair[0], keys], axis=0)
    value_span = jnp.concatenate([earlier_pair[1], values], axis=0)
    first = position * length
    outputs = []
    for block in range(length // WINDOW):
        query_block = queries[block * WINDOW : (block + 1) * WINDOW].reshape(
            WINDOW, local_heads, HD
        )
        key_block = key_span[block * WINDOW : block * WINDOW + 2 * WINDOW].reshape(
            2 * WINDOW, local_heads, HD
        )
        value_block = value_span[block * WINDOW : block * WINDOW + 2 * WINDOW].reshape(
            2 * WINDOW, local_heads, HD
        )
        query_pos = first + block * WINDOW + jnp.arange(WINDOW, dtype=jnp.int32)
        key_pos = first + (block - 1) * WINDOW + jnp.arange(2 * WINDOW, dtype=jnp.int32)
        valid = (
            (key_pos[None, :] <= query_pos[:, None])
            & (key_pos[None, :] > query_pos[:, None] - WINDOW)
            & (key_pos[None, :] >= 0)
        )
        scores = jnp.einsum(
            "qhd,khd->hqk", query_block, key_block, preferred_element_type=jnp.float32
        ) * HD ** (-0.5)
        weights = masked_softmax(scores, valid[None]).astype(jnp.bfloat16)
        mixed_block = jnp.einsum(
            "hqk,khd->qhd", weights, value_block, preferred_element_type=jnp.float32
        ).astype(jnp.bfloat16)
        outputs.append(mixed_block.reshape(WINDOW, local_width))
    heads_out = jnp.concatenate(outputs, axis=0)
    residual = residual + lax.psum_scatter(
        jnp.dot(heads_out, w_attn_out, preferred_element_type=jnp.float32).astype(jnp.bfloat16),
        "mp",
        scatter_dimension=0,
        tiled=True,
    ).astype(jnp.float32)
    normed = rms_scale(residual, norm_gains[1]).astype(jnp.bfloat16)
    mlp_in = lax.all_gather(normed, "mp", axis=0, tiled=True)
    gate = jnp.dot(
        mlp_in,
        full_gate,
        preferred_element_type=jnp.float32,
    )
    lifted = jnp.dot(
        mlp_in, full_up, preferred_element_type=jnp.float32
    )
    hidden = (jax.nn.silu(gate) * lifted).astype(jnp.bfloat16)
    down_terms = jnp.dot(
        hidden,
        full_down,
        preferred_element_type=jnp.float32,
    )
    residual = residual + lax.psum_scatter(
        down_terms.astype(jnp.bfloat16), "mp", scatter_dimension=0, tiled=True
    ).astype(jnp.float32)
    encoded = rms_scale(residual, norm_gains[2]).astype(jnp.bfloat16)
    states = lax.all_gather(encoded, "mp", axis=0, tiled=True)
    cross_keys = jnp.dot(states, w_cross_key, preferred_element_type=jnp.float32).astype(
        jnp.bfloat16
    )
    cross_values = jnp.dot(states, w_cross_value, preferred_element_type=jnp.float32).astype(
        jnp.bfloat16
    )
    following = passed_along(patch_start[:1], "seq", -1)
    last_end = jnp.where(position == seq_count - 1, seq_count * length, following[0])
    patch_end = jnp.concatenate([patch_start[1:], last_end[None]])
    patch_count = patch_start.shape[0]
    frame_states = padded(states, (("seq", 0),), REACH)
    margins = jnp.concatenate([frame_states[:REACH], frame_states[REACH + length :]], axis=0)
    margin_keys = jnp.dot(margins, w_cross_key, preferred_element_type=jnp.float32).astype(
        jnp.bfloat16
    )
    margin_values = jnp.dot(margins, w_cross_value, preferred_element_type=jnp.float32).astype(
        jnp.bfloat16
    )
    frame_keys = jnp.concatenate([margin_keys[:REACH], cross_keys, margin_keys[REACH:]], axis=0)
    frame_values = jnp.concatenate(
        [margin_values[:REACH], cross_values, margin_values[REACH:]], axis=0
    )
    frame_len = frame_states.shape[0]
    frame_pos = position * length - REACH + jnp.arange(frame_len, dtype=jnp.int32)
    member = (frame_pos[None, :] >= patch_start[:, None]) & (
        frame_pos[None, :] < patch_end[:, None]
    )
    counts = jnp.sum(member.astype(jnp.float32), axis=1)
    pooled = (
        jnp.dot(member.astype(jnp.bfloat16), frame_states, preferred_element_type=jnp.float32)
        / counts[:, None]
    )
    pooled_rows = pooled.astype(jnp.bfloat16)
    cross_queries = (
        jnp.dot(pooled_rows, w_cross_query, preferred_element_type=jnp.float32)
        .astype(jnp.bfloat16)
        .reshape(patch_count, local_heads, HD)
    )
    scores = jnp.einsum(
        "phd,khd->hpk",
        cross_queries,
        frame_keys.reshape(frame_len, local_heads, HD),
        preferred_element_type=jnp.float32,
    ) * HD ** (-0.5)
    weights = masked_softmax(scores, member[None]).astype(jnp.bfloat16)
    cross_heads = (
        jnp.einsum(
            "hpk,khd->phd",
            weights,
            frame_values.reshape(frame_len, local_heads, HD),
            preferred_element_type=jnp.float32,
        )
        .astype(jnp.bfloat16)
        .reshape(patch_count, local_width)
    )
    pooled, cross_heads = (pooled, cross_heads)
    own_share = jnp.dot(cross_heads, w_cross_out, preferred_element_type=jnp.float32).astype(
        jnp.bfloat16
    )
    mp_count = lax.axis_size("mp")
    mixed_patches = own_share.astype(jnp.float32)
    for step in range(1, mp_count):
        mixed_patches = mixed_patches + lax.ppermute(
            own_share, "mp", [(i, (i + step) % mp_count) for i in range(mp_count)]
        ).astype(jnp.float32)
    patch_hidden = (pooled + mixed_patches).astype(jnp.bfloat16)
    return jnp.dot(patch_hidden, w_global, preferred_element_type=jnp.float32).astype(jnp.bfloat16)


def solution(mesh):
    return jax.shard_map(
        per_device,
        mesh=mesh,
        in_specs=(
            P("seq"),
            P("seq", None),
            P("seq"),
            P("seq"),
            P(None, "mp"),
            P("seq", "mp"),
            P(),
            P(None, "mp"),
            P(None, "mp"),
            P(None, "mp"),
            P("mp", None),
            P("seq", "mp"),
            P("seq", "mp"),
            P("mp", "seq"),
            P(None, "mp"),
            P(None, "mp"),
            P(None, "mp"),
            P("mp", None),
            P(None, "mp"),
        ),
        out_specs=P("seq", "mp"),
        check_vma=False,
    )
```

```python
import jax
import jax.numpy as jnp
from jax import lax
from jax.sharding import PartitionSpec as P

HD = 64
WINDOW = 512
REACH = 512


def passed_along(value, axis, steps):
    count = lax.axis_size(axis)
    first, last = (max(0, -steps), min(count, count - steps))
    return lax.ppermute(value, axis, [(source, source + steps) for source in range(first, last)])


def padded(cells, sides, width):
    for axis, dim in sides:
        count = lax.axis_size(axis)
        ends = count - 1
        head = lax.slice_in_dim(cells, 0, width, axis=dim)
        tail = lax.slice_in_dim(cells, cells.shape[dim] - width, cells.shape[dim], axis=dim)
        cells = jnp.concatenate(
            [
                lax.ppermute(tail, axis, [(i, (i + 1) % count) for i in range(ends)]),
                cells,
                lax.ppermute(head, axis, [((i + 1) % count, i) for i in range(ends)]),
            ],
            axis=dim,
        )
    return cells


def rms_scale(values, gain):
    return values * lax.rsqrt(jnp.mean(values * values, axis=-1, keepdims=True) + 1e-05) * gain


def masked_softmax(scores, valid):
    scores = jnp.where(valid, scores, -1e30)
    highest = jnp.max(scores, axis=-1, keepdims=True)
    raised = jnp.exp(scores - highest)
    return raised / jnp.sum(raised, axis=-1, keepdims=True)


def spread_weights(own):
    count = lax.axis_size("seq")
    position = lax.axis_index("seq")
    pairs = count // 2
    near = [own]
    for step in range(1, pairs):
        near.append(lax.ppermute(own, "seq", [(i, (i + 2 * step) % count) for i in range(count)]))
    near = jnp.stack(near)
    far = lax.ppermute(near, "seq", [(i, i ^ 1) for i in range(count)])
    even = position % 2 == 0
    both = jnp.stack([jnp.where(even, near, far), jnp.where(even, far, near)], axis=1)
    ordered = jnp.stack(
        [
            lax.dynamic_index_in_dim(both, (position // 2 - i) % pairs, keepdims=False)
            for i in range(pairs)
        ]
    )
    return [
        ordered[:, :, part].reshape(count * own.shape[1], own.shape[2])
        for part in range(own.shape[0])
    ]


def per_device(
    byte_values,
    hash_owner,
    hash_slot,
    patch_start,
    byte_table,
    hash_table,
    norm_gains,
    w_query,
    w_key,
    w_value,
    w_attn_out,
    w_gate,
    w_up,
    w_down,
    w_cross_query,
    w_cross_key,
    w_cross_value,
    w_cross_out,
    w_global,
):
    seq_count = lax.axis_size("seq")
    position = lax.axis_index("seq")
    length = byte_values.shape[0]
    local_width = w_query.shape[1]
    local_heads = local_width // HD
    capacity = 2 * length // seq_count
    owner = hash_owner[:, 0]
    owner_hot = (owner[:, None] == jnp.arange(seq_count, dtype=jnp.int32)[None, :]).astype(
        jnp.bfloat16
    )
    line = jnp.arange(length, dtype=jnp.int32)
    earlier = (line[:, None] > line[None, :]).astype(jnp.bfloat16)
    before = jnp.dot(earlier, owner_hot, preferred_element_type=jnp.float32)
    order = jnp.sum(before * owner_hot.astype(jnp.float32), axis=1).astype(jnp.int32)
    target = owner * capacity + order
    chosen = (target[:, None] == jnp.arange(seq_count * capacity, dtype=jnp.int32)[None, :]).astype(
        jnp.bfloat16
    )
    digits = jnp.stack([hash_slot // 64, hash_slot % 64], axis=0).astype(jnp.bfloat16)
    asked = jnp.dot(digits, chosen, preferred_element_type=jnp.float32).astype(jnp.int32)
    requests = (asked[0] * 64 + asked[1]).reshape(seq_count, capacity)
    wanted = lax.all_to_all(requests, "seq", split_axis=0, concat_axis=0, tiled=True).reshape(-1)
    picked = (
        wanted[:, None] == jnp.arange(hash_table.shape[0], dtype=jnp.int32)[None, :]
    ).astype(jnp.bfloat16)
    found = jnp.dot(picked, hash_table, preferred_element_type=jnp.float32).astype(jnp.bfloat16)
    fetched = lax.all_to_all(
        found.reshape(seq_count, capacity, -1), "seq", split_axis=0, concat_axis=0, tiled=True
    ).reshape(seq_count * capacity, -1)
    hash_rows = jnp.dot(chosen, fetched, preferred_element_type=jnp.float32)
    byte_hot = (byte_values[:, None] == jnp.arange(256, dtype=jnp.int32)[None, :]).astype(
        jnp.bfloat16
    )
    byte_rows = jnp.dot(byte_hot, byte_table, preferred_element_type=jnp.float32)
    embed = (byte_rows + hash_rows).astype(jnp.bfloat16)
    packed = jnp.stack([w_gate, w_up, w_down.T])
    embed, packed = lax.optimization_barrier((embed, packed))
    full_gate, full_up, full_down = spread_weights(packed)
    embed_parts = lax.all_gather(embed, "mp", axis=0, tiled=False)
    embed_full = jnp.concatenate(
        [embed_parts[i] for i in range(embed_parts.shape[0])], axis=1
    )
    mp_count = lax.axis_size("mp")
    share = WINDOW // mp_count
    residuals = [
        lax.dynamic_slice_in_dim(
            embed_full, block * WINDOW + lax.axis_index("mp") * share, share, axis=0
        ).astype(jnp.float32)
        for block in range(length // WINDOW)
    ]
    layer_in = rms_scale(embed_full.astype(jnp.float32), norm_gains[0]).astype(jnp.bfloat16)
    layer_in, full_gate, full_up, full_down = lax.optimization_barrier(
        (layer_in, full_gate, full_up, full_down)
    )
    queries = jnp.dot(layer_in, w_query, preferred_element_type=jnp.float32).astype(jnp.bfloat16)
    keys = jnp.dot(layer_in, w_key, preferred_element_type=jnp.float32).astype(jnp.bfloat16)
    values = jnp.dot(layer_in, w_value, preferred_element_type=jnp.float32).astype(jnp.bfloat16)
    paired = jnp.stack([keys, values])
    earlier_pair = passed_along(paired[:, length - WINDOW :], "seq", 1)
    key_span = jnp.concatenate([earlier_pair[0], keys], axis=0)
    value_span = jnp.concatenate([earlier_pair[1], values], axis=0)
    first = position * length
    for block in range(length // WINDOW):
        query_block = queries[block * WINDOW : (block + 1) * WINDOW].reshape(
            WINDOW, local_heads, HD
        )
        key_block = key_span[block * WINDOW : block * WINDOW + 2 * WINDOW].reshape(
            2 * WINDOW, local_heads, HD
        )
        value_block = value_span[block * WINDOW : block * WINDOW + 2 * WINDOW].reshape(
            2 * WINDOW, local_heads, HD
        )
        query_pos = first + block * WINDOW + jnp.arange(WINDOW, dtype=jnp.int32)
        key_pos = first + (block - 1) * WINDOW + jnp.arange(2 * WINDOW, dtype=jnp.int32)
        valid = (
            (key_pos[None, :] <= query_pos[:, None])
            & (key_pos[None, :] > query_pos[:, None] - WINDOW)
            & (key_pos[None, :] >= 0)
        )
        scores = jnp.einsum(
            "qhd,khd->hqk", query_block, key_block, preferred_element_type=jnp.float32
        ) * HD ** (-0.5)
        weights = masked_softmax(scores, valid[None]).astype(jnp.bfloat16)
        mixed_block = jnp.einsum(
            "hqk,khd->qhd", weights, value_block, preferred_element_type=jnp.float32
        ).astype(jnp.bfloat16)
        heads_out = mixed_block.reshape(WINDOW, local_width)
        attn_terms = jnp.dot(heads_out, w_attn_out, preferred_element_type=jnp.float32)
        residuals[block] = residuals[block] + lax.psum_scatter(
            attn_terms.astype(jnp.bfloat16), "mp", scatter_dimension=0, tiled=True
        ).astype(jnp.float32)
    gathered = []
    for block, residual in enumerate(residuals):
        if block > 0:
            residual, normed = lax.optimization_barrier((residual, normed))
            residuals[block] = residual
        normed = rms_scale(residual, norm_gains[1]).astype(jnp.bfloat16)
        gathered.append(lax.all_gather(normed, "mp", axis=0, tiled=True))
    encoded_blocks = []
    for block, (residual, mlp_in) in enumerate(zip(residuals, gathered)):
        gate = jnp.dot(mlp_in, full_gate, preferred_element_type=jnp.float32)
        lifted = jnp.dot(mlp_in, full_up, preferred_element_type=jnp.float32)
        hidden = (jax.nn.silu(gate) * lifted).astype(jnp.bfloat16)
        down_terms = lax.dot_general(
            hidden, full_down, (((1,), (1,)), ((), ())), preferred_element_type=jnp.float32
        )
        residual = residual + lax.psum_scatter(
            down_terms.astype(jnp.bfloat16), "mp", scatter_dimension=0, tiled=True
        ).astype(jnp.float32)
        if block > 0:
            residual, encoded_blocks[-1] = lax.optimization_barrier((residual, encoded_blocks[-1]))
        encoded_blocks.append(rms_scale(residual, norm_gains[2]).astype(jnp.bfloat16))
    state_blocks = [lax.all_gather(block, "mp", axis=0, tiled=True) for block in encoded_blocks]
    states = jnp.concatenate(state_blocks, axis=0)
    cross_keys = jnp.concatenate(
        [
            jnp.dot(block, w_cross_key, preferred_element_type=jnp.float32).astype(jnp.bfloat16)
            for block in state_blocks
        ]
    )
    cross_values = jnp.concatenate(
        [
            jnp.dot(block, w_cross_value, preferred_element_type=jnp.float32).astype(jnp.bfloat16)
            for block in state_blocks
        ]
    )
    following = passed_along(patch_start[:1], "seq", -1)
    last_end = jnp.where(position == seq_count - 1, seq_count * length, following[0])
    patch_end = jnp.concatenate([patch_start[1:], last_end[None]])
    patch_count = patch_start.shape[0]
    frame_states = padded(states, (("seq", 0),), REACH)
    margins = jnp.concatenate([frame_states[:REACH], frame_states[REACH + length :]], axis=0)
    margin_keys = jnp.dot(margins, w_cross_key, preferred_element_type=jnp.float32).astype(
        jnp.bfloat16
    )
    margin_values = jnp.dot(margins, w_cross_value, preferred_element_type=jnp.float32).astype(
        jnp.bfloat16
    )
    frame_keys = jnp.concatenate([margin_keys[:REACH], cross_keys, margin_keys[REACH:]], axis=0)
    frame_values = jnp.concatenate(
        [margin_values[:REACH], cross_values, margin_values[REACH:]], axis=0
    )
    frame_len = frame_states.shape[0]
    frame_pos = position * length - REACH + jnp.arange(frame_len, dtype=jnp.int32)
    member = (frame_pos[None, :] >= patch_start[:, None]) & (
        frame_pos[None, :] < patch_end[:, None]
    )
    counts = jnp.sum(member.astype(jnp.float32), axis=1)
    pooled = (
        jnp.dot(member.astype(jnp.bfloat16), frame_states, preferred_element_type=jnp.float32)
        / counts[:, None]
    )
    pooled_rows = pooled.astype(jnp.bfloat16)
    cross_queries = (
        jnp.dot(pooled_rows, w_cross_query, preferred_element_type=jnp.float32)
        .astype(jnp.bfloat16)
        .reshape(patch_count, local_heads, HD)
    )
    scores = jnp.einsum(
        "phd,khd->hpk",
        cross_queries,
        frame_keys.reshape(frame_len, local_heads, HD),
        preferred_element_type=jnp.float32,
    ) * HD ** (-0.5)
    weights = masked_softmax(scores, member[None]).astype(jnp.bfloat16)
    cross_heads = (
        jnp.einsum(
            "hpk,khd->phd",
            weights,
            frame_values.reshape(frame_len, local_heads, HD),
            preferred_element_type=jnp.float32,
        )
        .astype(jnp.bfloat16)
        .reshape(patch_count, local_width)
    )
    pooled, cross_heads = (pooled, cross_heads)
    own_share = jnp.dot(cross_heads, w_cross_out, preferred_element_type=jnp.float32).astype(
        jnp.bfloat16
    )
    mixed_patches = own_share.astype(jnp.float32)
    for step in range(1, mp_count):
        mixed_patches = mixed_patches + lax.ppermute(
            own_share, "mp", [(i, (i + step) % mp_count) for i in range(mp_count)]
        ).astype(jnp.float32)
    patch_hidden = (pooled + mixed_patches).astype(jnp.bfloat16)
    return jnp.dot(patch_hidden, w_global, preferred_element_type=jnp.float32).astype(jnp.bfloat16)


def solution(mesh):
    return jax.shard_map(
        per_device,
        mesh=mesh,
        in_specs=(
            P("seq"),
            P("seq", None),
            P("seq"),
            P("seq"),
            P(None, "mp"),
            P("seq", "mp"),
            P(),
            P(None, "mp"),
            P(None, "mp"),
            P(None, "mp"),
            P("mp", None),
            P("seq", "mp"),
            P("seq", "mp"),
            P("mp", "seq"),
            P(None, "mp"),
            P(None, "mp"),
            P(None, "mp"),
            P("mp", None),
            P(None, "mp"),
        ),
        out_specs=P("seq", "mp"),
        check_vma=False,
    )
```

```python
import jax
import jax.numpy as jnp
from jax import lax
from jax.sharding import PartitionSpec as P

HD = 64
WINDOW = 512
REACH = 512


def passed_along(value, axis, steps):
    count = lax.axis_size(axis)
    first, last = (max(0, -steps), min(count, count - steps))
    return lax.ppermute(value, axis, [(source, source + steps) for source in range(first, last)])


def padded(cells, sides, width):
    for axis, dim in sides:
        count = lax.axis_size(axis)
        ends = count - 1
        head = lax.slice_in_dim(cells, 0, width, axis=dim)
        tail = lax.slice_in_dim(cells, cells.shape[dim] - width, cells.shape[dim], axis=dim)
        cells = jnp.concatenate(
            [
                lax.ppermute(tail, axis, [(i, (i + 1) % count) for i in range(ends)]),
                cells,
                lax.ppermute(head, axis, [((i + 1) % count, i) for i in range(ends)]),
            ],
            axis=dim,
        )
    return cells


def rms_scale(values, gain):
    return values * lax.rsqrt(jnp.mean(values * values, axis=-1, keepdims=True) + 1e-05) * gain


def masked_softmax(scores, valid):
    scores = jnp.where(valid, scores, -1e30)
    highest = jnp.max(scores, axis=-1, keepdims=True)
    raised = jnp.exp(scores - highest)
    return raised / jnp.sum(raised, axis=-1, keepdims=True)


def spread_weights(own):
    count = lax.axis_size("seq")
    position = lax.axis_index("seq")
    pairs = count // 2
    near = [own]
    for step in range(1, pairs):
        near.append(lax.ppermute(own, "seq", [(i, (i + 2 * step) % count) for i in range(count)]))
    near = jnp.stack(near)
    far = lax.ppermute(near, "seq", [(i, i ^ 1) for i in range(count)])
    even = position % 2 == 0
    both = jnp.stack([jnp.where(even, near, far), jnp.where(even, far, near)], axis=1)
    ordered = jnp.stack(
        [
            lax.dynamic_index_in_dim(both, (position // 2 - i) % pairs, keepdims=False)
            for i in range(pairs)
        ]
    )
    return [
        ordered[:, :, part].reshape(count * own.shape[1], own.shape[2])
        for part in range(own.shape[0])
    ]


def after(value, *others):
    return lax.optimization_barrier((value, *others))[0]


def per_device(
    byte_values,
    hash_owner,
    hash_slot,
    patch_start,
    byte_table,
    hash_table,
    norm_gains,
    w_query,
    w_key,
    w_value,
    w_attn_out,
    w_gate,
    w_up,
    w_down,
    w_cross_query,
    w_cross_key,
    w_cross_value,
    w_cross_out,
    w_global,
):
    seq_count = lax.axis_size("seq")
    position = lax.axis_index("seq")
    length = byte_values.shape[0]
    local_width = w_query.shape[1]
    local_heads = local_width // HD
    capacity = 2 * length // seq_count
    owner = hash_owner[:, 0]
    owner_hot = (owner[:, None] == jnp.arange(seq_count, dtype=jnp.int32)[None, :]).astype(
        jnp.bfloat16
    )
    line = jnp.arange(length, dtype=jnp.int32)
    earlier = (line[:, None] > line[None, :]).astype(jnp.bfloat16)
    before = jnp.dot(earlier, owner_hot, preferred_element_type=jnp.float32)
    order = jnp.sum(before * owner_hot.astype(jnp.float32), axis=1).astype(jnp.int32)
    target = owner * capacity + order
    chosen = (target[:, None] == jnp.arange(seq_count * capacity, dtype=jnp.int32)[None, :]).astype(
        jnp.bfloat16
    )
    digits = jnp.stack([hash_slot // 64, hash_slot % 64], axis=0).astype(jnp.bfloat16)
    asked = jnp.dot(digits, chosen, preferred_element_type=jnp.float32).astype(jnp.int32)
    requests = (asked[0] * 64 + asked[1]).reshape(seq_count, capacity)
    wanted = lax.all_to_all(requests, "seq", split_axis=0, concat_axis=0, tiled=True).reshape(-1)
    picked = (
        wanted[:, None] == jnp.arange(hash_table.shape[0], dtype=jnp.int32)[None, :]
    ).astype(jnp.bfloat16)
    found = jnp.dot(picked, hash_table, preferred_element_type=jnp.float32).astype(jnp.bfloat16)
    fetched = lax.all_to_all(
        found.reshape(seq_count, capacity, -1), "seq", split_axis=0, concat_axis=0, tiled=True
    ).reshape(seq_count * capacity, -1)
    hash_rows = jnp.dot(chosen, fetched, preferred_element_type=jnp.float32)
    byte_hot = (byte_values[:, None] == jnp.arange(256, dtype=jnp.int32)[None, :]).astype(
        jnp.bfloat16
    )
    byte_rows = jnp.dot(byte_hot, byte_table, preferred_element_type=jnp.float32)
    embed = (byte_rows + hash_rows).astype(jnp.bfloat16)
    packed = jnp.stack([w_gate, w_up, w_down.T])
    embed, packed = lax.optimization_barrier((embed, packed))
    full_gate, full_up, full_down = spread_weights(packed)
    embed_parts = lax.all_gather(embed, "mp", axis=0, tiled=False)
    embed_full = jnp.concatenate(
        [embed_parts[i] for i in range(embed_parts.shape[0])], axis=1
    )
    mp_count = lax.axis_size("mp")
    share = WINDOW // mp_count
    residuals = [
        lax.dynamic_slice_in_dim(
            embed_full, block * WINDOW + lax.axis_index("mp") * share, share, axis=0
        ).astype(jnp.float32)
        for block in range(length // WINDOW)
    ]
    layer_in = rms_scale(embed_full.astype(jnp.float32), norm_gains[0]).astype(jnp.bfloat16)
    layer_in, full_gate, full_up, full_down = lax.optimization_barrier(
        (layer_in, full_gate, full_up, full_down)
    )
    queries = jnp.dot(layer_in, w_query, preferred_element_type=jnp.float32).astype(jnp.bfloat16)
    keys = jnp.dot(layer_in, w_key, preferred_element_type=jnp.float32).astype(jnp.bfloat16)
    values = jnp.dot(layer_in, w_value, preferred_element_type=jnp.float32).astype(jnp.bfloat16)
    paired = jnp.stack([keys, values])
    earlier_pair = passed_along(paired[:, length - WINDOW :], "seq", 1)
    key_span = jnp.concatenate([earlier_pair[0], keys], axis=0)
    value_span = jnp.concatenate([earlier_pair[1], values], axis=0)
    first = position * length
    terms = []
    scattered = []
    for block in range(length // WINDOW):
        query_block = queries[block * WINDOW : (block + 1) * WINDOW].reshape(
            WINDOW, local_heads, HD
        )
        key_block = key_span[block * WINDOW : block * WINDOW + 2 * WINDOW].reshape(
            2 * WINDOW, local_heads, HD
        )
        value_block = value_span[block * WINDOW : block * WINDOW + 2 * WINDOW].reshape(
            2 * WINDOW, local_heads, HD
        )
        query_block = after(query_block, *terms[-1:])
        query_pos = first + block * WINDOW + jnp.arange(WINDOW, dtype=jnp.int32)
        key_pos = first + (block - 1) * WINDOW + jnp.arange(2 * WINDOW, dtype=jnp.int32)
        valid = (
            (key_pos[None, :] <= query_pos[:, None])
            & (key_pos[None, :] > query_pos[:, None] - WINDOW)
            & (key_pos[None, :] >= 0)
        )
        scores = jnp.einsum(
            "qhd,khd->hqk", query_block, key_block, preferred_element_type=jnp.float32
        ) * HD ** (-0.5)
        weights = masked_softmax(scores, valid[None]).astype(jnp.bfloat16)
        mixed_block = jnp.einsum(
            "hqk,khd->qhd", weights, value_block, preferred_element_type=jnp.float32
        ).astype(jnp.bfloat16)
        heads_out = mixed_block.reshape(WINDOW, local_width)
        attn_terms = jnp.dot(
            heads_out, w_attn_out, preferred_element_type=jnp.float32
        ).astype(jnp.bfloat16)
        terms.append(attn_terms)
        scattered.append(
            lax.psum_scatter(attn_terms, "mp", scatter_dimension=0, tiled=True)
        )
    gathered = []
    norms = []
    for block, residual in enumerate(residuals):
        mixed = after(scattered[block], terms[-1], *norms[-1:])
        residuals[block] = residual + mixed.astype(jnp.float32)
        norms.append(rms_scale(residuals[block], norm_gains[1]).astype(jnp.bfloat16))
        gathered.append(lax.all_gather(norms[block], "mp", axis=0, tiled=True))
    terms = []
    scattered = []
    for mlp_in in gathered:
        mlp_in = after(mlp_in, norms[-1], *terms[-1:])
        gate = jnp.dot(mlp_in, full_gate, preferred_element_type=jnp.float32)
        lifted = jnp.dot(mlp_in, full_up, preferred_element_type=jnp.float32)
        hidden = (jax.nn.silu(gate) * lifted).astype(jnp.bfloat16)
        down_terms = lax.dot_general(
            hidden, full_down, (((1,), (1,)), ((), ())), preferred_element_type=jnp.float32
        ).astype(jnp.bfloat16)
        terms.append(down_terms)
        scattered.append(
            lax.psum_scatter(down_terms, "mp", scatter_dimension=0, tiled=True)
        )
    encoded_blocks = []
    for residual, mixed in zip(residuals, scattered):
        mixed = after(mixed, terms[-1], *encoded_blocks[-1:])
        residual = residual + mixed.astype(jnp.float32)
        encoded_blocks.append(rms_scale(residual, norm_gains[2]).astype(jnp.bfloat16))
    state_blocks = []
    key_parts = []
    value_parts = []
    for block in encoded_blocks:
        state = lax.all_gather(block, "mp", axis=0, tiled=True)
        state = after(state, encoded_blocks[-1], *key_parts[-1:], *value_parts[-1:])
        state_blocks.append(state)
        key_parts.append(
            jnp.dot(state, w_cross_key, preferred_element_type=jnp.float32).astype(jnp.bfloat16)
        )
        value_parts.append(
            jnp.dot(state, w_cross_value, preferred_element_type=jnp.float32).astype(jnp.bfloat16)
        )
    states = jnp.concatenate(state_blocks, axis=0)
    cross_keys = jnp.concatenate(key_parts, axis=0)
    cross_values = jnp.concatenate(value_parts, axis=0)
    following = passed_along(patch_start[:1], "seq", -1)
    last_end = jnp.where(position == seq_count - 1, seq_count * length, following[0])
    patch_end = jnp.concatenate([patch_start[1:], last_end[None]])
    patch_count = patch_start.shape[0]
    frame_states = padded(states, (("seq", 0),), REACH)
    margins = jnp.concatenate([frame_states[:REACH], frame_states[REACH + length :]], axis=0)
    margin_keys = jnp.dot(margins, w_cross_key, preferred_element_type=jnp.float32).astype(
        jnp.bfloat16
    )
    margin_values = jnp.dot(margins, w_cross_value, preferred_element_type=jnp.float32).astype(
        jnp.bfloat16
    )
    frame_keys = jnp.concatenate([margin_keys[:REACH], cross_keys, margin_keys[REACH:]], axis=0)
    frame_values = jnp.concatenate(
        [margin_values[:REACH], cross_values, margin_values[REACH:]], axis=0
    )
    frame_len = frame_states.shape[0]
    frame_pos = position * length - REACH + jnp.arange(frame_len, dtype=jnp.int32)
    member = (frame_pos[None, :] >= patch_start[:, None]) & (
        frame_pos[None, :] < patch_end[:, None]
    )
    counts = jnp.sum(member.astype(jnp.float32), axis=1)
    pooled = (
        jnp.dot(member.astype(jnp.bfloat16), frame_states, preferred_element_type=jnp.float32)
        / counts[:, None]
    )
    pooled_rows = pooled.astype(jnp.bfloat16)
    cross_queries = (
        jnp.dot(pooled_rows, w_cross_query, preferred_element_type=jnp.float32)
        .astype(jnp.bfloat16)
        .reshape(patch_count, local_heads, HD)
    )
    scores = jnp.einsum(
        "phd,khd->hpk",
        cross_queries,
        frame_keys.reshape(frame_len, local_heads, HD),
        preferred_element_type=jnp.float32,
    ) * HD ** (-0.5)
    weights = masked_softmax(scores, member[None]).astype(jnp.bfloat16)
    cross_heads = (
        jnp.einsum(
            "hpk,khd->phd",
            weights,
            frame_values.reshape(frame_len, local_heads, HD),
            preferred_element_type=jnp.float32,
        )
        .astype(jnp.bfloat16)
        .reshape(patch_count, local_width)
    )
    pooled, cross_heads = (pooled, cross_heads)
    own_share = jnp.dot(cross_heads, w_cross_out, preferred_element_type=jnp.float32).astype(
        jnp.bfloat16
    )
    mixed_patches = own_share.astype(jnp.float32)
    for step in range(1, mp_count):
        mixed_patches = mixed_patches + lax.ppermute(
            own_share, "mp", [(i, (i + step) % mp_count) for i in range(mp_count)]
        ).astype(jnp.float32)
    patch_hidden = (pooled + mixed_patches).astype(jnp.bfloat16)
    return jnp.dot(patch_hidden, w_global, preferred_element_type=jnp.float32).astype(jnp.bfloat16)


def solution(mesh):
    return jax.shard_map(
        per_device,
        mesh=mesh,
        in_specs=(
            P("seq"),
            P("seq", None),
            P("seq"),
            P("seq"),
            P(None, "mp"),
            P("seq", "mp"),
            P(),
            P(None, "mp"),
            P(None, "mp"),
            P(None, "mp"),
            P("mp", None),
            P("seq", "mp"),
            P("seq", "mp"),
            P("mp", "seq"),
            P(None, "mp"),
            P(None, "mp"),
            P(None, "mp"),
            P("mp", None),
            P(None, "mp"),
        ),
        out_specs=P("seq", "mp"),
        check_vma=False,
    )
```

```python
import jax
import jax.numpy as jnp
from jax import lax
from jax.sharding import PartitionSpec as P

HD = 64
WINDOW = 512
REACH = 512


def passed_along(value, axis, steps):
    count = lax.axis_size(axis)
    first, last = (max(0, -steps), min(count, count - steps))
    return lax.ppermute(value, axis, [(source, source + steps) for source in range(first, last)])


def padded(cells, sides, width):
    for axis, dim in sides:
        count = lax.axis_size(axis)
        ends = count - 1
        head = lax.slice_in_dim(cells, 0, width, axis=dim)
        tail = lax.slice_in_dim(cells, cells.shape[dim] - width, cells.shape[dim], axis=dim)
        cells = jnp.concatenate(
            [
                lax.ppermute(tail, axis, [(i, (i + 1) % count) for i in range(ends)]),
                cells,
                lax.ppermute(head, axis, [((i + 1) % count, i) for i in range(ends)]),
            ],
            axis=dim,
        )
    return cells


def rms_scale(values, gain):
    return values * lax.rsqrt(jnp.mean(values * values, axis=-1, keepdims=True) + 1e-05) * gain


def masked_softmax(scores, valid):
    scores = jnp.where(valid, scores, -1e30)
    highest = jnp.max(scores, axis=-1, keepdims=True)
    raised = jnp.exp(scores - highest)
    return raised / jnp.sum(raised, axis=-1, keepdims=True)


def spread_weights(own):
    count = lax.axis_size("seq")
    near = [own]
    for step in range(1, count // 2):
        near.append(lax.ppermute(own, "seq", [(i, (i + 2 * step) % count) for i in range(count)]))
    near = jnp.stack(near)
    return near, lax.ppermute(near, "seq", [(i, i ^ 1) for i in range(count)])


def ordered_weights(near, far):
    position = lax.axis_index("seq")
    pairs, parts, rows, width = near.shape
    even = position % 2 == 0
    both = jnp.stack([jnp.where(even, near, far), jnp.where(even, far, near)], axis=1)
    ordered = jnp.stack(
        [
            lax.dynamic_index_in_dim(both, (position // 2 - i) % pairs, keepdims=False)
            for i in range(pairs)
        ]
    )
    return [ordered[:, :, part].reshape(pairs * 2 * rows, width) for part in range(parts)]


def per_device(
    byte_values,
    hash_owner,
    hash_slot,
    patch_start,
    byte_table,
    hash_table,
    norm_gains,
    w_query,
    w_key,
    w_value,
    w_attn_out,
    w_gate,
    w_up,
    w_down,
    w_cross_query,
    w_cross_key,
    w_cross_value,
    w_cross_out,
    w_global,
):
    seq_count = lax.axis_size("seq")
    position = lax.axis_index("seq")
    length = byte_values.shape[0]
    local_width = w_query.shape[1]
    local_heads = local_width // HD
    capacity = 2 * length // seq_count
    owner = hash_owner[:, 0]
    owner_hot = (owner[:, None] == jnp.arange(seq_count, dtype=jnp.int32)[None, :]).astype(
        jnp.bfloat16
    )
    line = jnp.arange(length, dtype=jnp.int32)
    earlier = (line[:, None] > line[None, :]).astype(jnp.bfloat16)
    before = jnp.dot(earlier, owner_hot, preferred_element_type=jnp.float32)
    order = jnp.sum(before * owner_hot.astype(jnp.float32), axis=1).astype(jnp.int32)
    target = owner * capacity + order
    chosen = (target[:, None] == jnp.arange(seq_count * capacity, dtype=jnp.int32)[None, :]).astype(
        jnp.bfloat16
    )
    digits = jnp.stack([hash_slot // 64, hash_slot % 64], axis=0).astype(jnp.bfloat16)
    asked = jnp.dot(digits, chosen, preferred_element_type=jnp.float32).astype(jnp.int32)
    requests = (asked[0] * 64 + asked[1]).reshape(seq_count, capacity)
    wanted = lax.all_to_all(requests, "seq", split_axis=0, concat_axis=0, tiled=True).reshape(-1)
    picked = (
        wanted[:, None] == jnp.arange(hash_table.shape[0], dtype=jnp.int32)[None, :]
    ).astype(jnp.bfloat16)
    found = jnp.dot(picked, hash_table, preferred_element_type=jnp.float32).astype(jnp.bfloat16)
    fetched = lax.all_to_all(
        found.reshape(seq_count, capacity, -1), "seq", split_axis=0, concat_axis=0, tiled=True
    ).reshape(seq_count * capacity, -1)
    hash_rows = jnp.dot(chosen, fetched, preferred_element_type=jnp.float32)
    byte_hot = (byte_values[:, None] == jnp.arange(256, dtype=jnp.int32)[None, :]).astype(
        jnp.bfloat16
    )
    byte_rows = jnp.dot(byte_hot, byte_table, preferred_element_type=jnp.float32)
    embed = (byte_rows + hash_rows).astype(jnp.bfloat16)
    packed = jnp.stack([w_gate, w_up, w_down.T])
    embed, packed = lax.optimization_barrier((embed, packed))
    near, far = spread_weights(packed)
    embed_parts = lax.all_gather(embed, "mp", axis=0, tiled=False)
    embed_full = jnp.concatenate(
        [embed_parts[i] for i in range(embed_parts.shape[0])], axis=1
    )
    share = length // lax.axis_size("mp")
    residual = lax.dynamic_slice_in_dim(
        embed_full, lax.axis_index("mp") * share, share, axis=0
    ).astype(jnp.float32)
    layer_in = rms_scale(embed_full.astype(jnp.float32), norm_gains[0]).astype(jnp.bfloat16)
    queries = jnp.dot(layer_in, w_query, preferred_element_type=jnp.float32).astype(jnp.bfloat16)
    keys = jnp.dot(layer_in, w_key, preferred_element_type=jnp.float32).astype(jnp.bfloat16)
    values = jnp.dot(layer_in, w_value, preferred_element_type=jnp.float32).astype(jnp.bfloat16)
    paired = jnp.stack([keys, values])
    earlier_pair = passed_along(paired[:, length - WINDOW :], "seq", 1)
    key_span = jnp.concatenate([earlier_pair[0], keys], axis=0)
    value_span = jnp.concatenate([earlier_pair[1], values], axis=0)
    first = position * length
    outputs = []
    for block in range(length // WINDOW):
        query_block = queries[block * WINDOW : (block + 1) * WINDOW].reshape(
            WINDOW, local_heads, HD
        )
        key_block = key_span[block * WINDOW : block * WINDOW + 2 * WINDOW].reshape(
            2 * WINDOW, local_heads, HD
        )
        value_block = value_span[block * WINDOW : block * WINDOW + 2 * WINDOW].reshape(
            2 * WINDOW, local_heads, HD
        )
        query_pos = first + block * WINDOW + jnp.arange(WINDOW, dtype=jnp.int32)
        key_pos = first + (block - 1) * WINDOW + jnp.arange(2 * WINDOW, dtype=jnp.int32)
        valid = (
            (key_pos[None, :] <= query_pos[:, None])
            & (key_pos[None, :] > query_pos[:, None] - WINDOW)
            & (key_pos[None, :] >= 0)
        )
        scores = jnp.einsum(
            "qhd,khd->hqk", query_block, key_block, preferred_element_type=jnp.float32
        ) * HD ** (-0.5)
        weights = masked_softmax(scores, valid[None]).astype(jnp.bfloat16)
        mixed_block = jnp.einsum(
            "hqk,khd->qhd", weights, value_block, preferred_element_type=jnp.float32
        ).astype(jnp.bfloat16)
        outputs.append(mixed_block.reshape(WINDOW, local_width))
    heads_out = jnp.concatenate(outputs, axis=0)
    attn_terms = jnp.dot(heads_out, w_attn_out, preferred_element_type=jnp.float32).astype(
        jnp.bfloat16
    )
    near, far, _ = lax.optimization_barrier((near, far, attn_terms))
    full_gate, full_up, full_down = ordered_weights(near, far)
    residual = residual + lax.psum_scatter(
        attn_terms, "mp", scatter_dimension=0, tiled=True
    ).astype(jnp.float32)
    normed = rms_scale(residual, norm_gains[1]).astype(jnp.bfloat16)
    mlp_in = lax.all_gather(normed, "mp", axis=0, tiled=True)
    gate = jnp.dot(
        mlp_in,
        full_gate,
        preferred_element_type=jnp.float32,
    )
    lifted = jnp.dot(
        mlp_in, full_up, preferred_element_type=jnp.float32
    )
    hidden = (jax.nn.silu(gate) * lifted).astype(jnp.bfloat16)
    down_terms = lax.dot_general(
        hidden, full_down, (((1,), (1,)), ((), ())), preferred_element_type=jnp.float32
    )
    residual = residual + lax.psum_scatter(
        down_terms.astype(jnp.bfloat16), "mp", scatter_dimension=0, tiled=True
    ).astype(jnp.float32)
    encoded = rms_scale(residual, norm_gains[2]).astype(jnp.bfloat16)
    states = lax.all_gather(encoded, "mp", axis=0, tiled=True)
    cross_keys = jnp.dot(states, w_cross_key, preferred_element_type=jnp.float32).astype(
        jnp.bfloat16
    )
    cross_values = jnp.dot(states, w_cross_value, preferred_element_type=jnp.float32).astype(
        jnp.bfloat16
    )
    following = passed_along(patch_start[:1], "seq", -1)
    last_end = jnp.where(position == seq_count - 1, seq_count * length, following[0])
    patch_end = jnp.concatenate([patch_start[1:], last_end[None]])
    patch_count = patch_start.shape[0]
    frame_states = padded(states, (("seq", 0),), REACH)
    margins = jnp.concatenate([frame_states[:REACH], frame_states[REACH + length :]], axis=0)
    margin_keys = jnp.dot(margins, w_cross_key, preferred_element_type=jnp.float32).astype(
        jnp.bfloat16
    )
    margin_values = jnp.dot(margins, w_cross_value, preferred_element_type=jnp.float32).astype(
        jnp.bfloat16
    )
    frame_keys = jnp.concatenate([margin_keys[:REACH], cross_keys, margin_keys[REACH:]], axis=0)
    frame_values = jnp.concatenate(
        [margin_values[:REACH], cross_values, margin_values[REACH:]], axis=0
    )
    frame_len = frame_states.shape[0]
    frame_pos = position * length - REACH + jnp.arange(frame_len, dtype=jnp.int32)
    member = (frame_pos[None, :] >= patch_start[:, None]) & (
        frame_pos[None, :] < patch_end[:, None]
    )
    counts = jnp.sum(member.astype(jnp.float32), axis=1)
    pooled = (
        jnp.dot(member.astype(jnp.bfloat16), frame_states, preferred_element_type=jnp.float32)
        / counts[:, None]
    )
    pooled_rows = pooled.astype(jnp.bfloat16)
    cross_queries = (
        jnp.dot(pooled_rows, w_cross_query, preferred_element_type=jnp.float32)
        .astype(jnp.bfloat16)
        .reshape(patch_count, local_heads, HD)
    )
    scores = jnp.einsum(
        "phd,khd->hpk",
        cross_queries,
        frame_keys.reshape(frame_len, local_heads, HD),
        preferred_element_type=jnp.float32,
    ) * HD ** (-0.5)
    weights = masked_softmax(scores, member[None]).astype(jnp.bfloat16)
    cross_heads = (
        jnp.einsum(
            "hpk,khd->phd",
            weights,
            frame_values.reshape(frame_len, local_heads, HD),
            preferred_element_type=jnp.float32,
        )
        .astype(jnp.bfloat16)
        .reshape(patch_count, local_width)
    )
    pooled, cross_heads = (pooled, cross_heads)
    own_share = jnp.dot(cross_heads, w_cross_out, preferred_element_type=jnp.float32).astype(
        jnp.bfloat16
    )
    mp_count = lax.axis_size("mp")
    mixed_patches = own_share.astype(jnp.float32)
    for step in range(1, mp_count):
        mixed_patches = mixed_patches + lax.ppermute(
            own_share, "mp", [(i, (i + step) % mp_count) for i in range(mp_count)]
        ).astype(jnp.float32)
    patch_hidden = (pooled + mixed_patches).astype(jnp.bfloat16)
    return jnp.dot(patch_hidden, w_global, preferred_element_type=jnp.float32).astype(jnp.bfloat16)


def solution(mesh):
    return jax.shard_map(
        per_device,
        mesh=mesh,
        in_specs=(
            P("seq"),
            P("seq", None),
            P("seq"),
            P("seq"),
            P(None, "mp"),
            P("seq", "mp"),
            P(),
            P(None, "mp"),
            P(None, "mp"),
            P(None, "mp"),
            P("mp", None),
            P("seq", "mp"),
            P("seq", "mp"),
            P("mp", "seq"),
            P(None, "mp"),
            P(None, "mp"),
            P(None, "mp"),
            P("mp", None),
            P(None, "mp"),
        ),
        out_specs=P("seq", "mp"),
        check_vma=False,
    )
```
